32 devices in a mesh: groups: 2 (over y), gx: 4 (over x, core), gy: 4 (over z).
Axes of the slice: x: 2, y: 2, z: 4, core: 2. Of those that a mesh axis runs over, the one named last changes fastest.
Arguments:
- activations: bfloat16 [128, 18432], P(('groups', 'gy'), 'gx'), parts along dimension 0, may hold values from -6 to 6
- query_weight: bfloat16 [18432, 6144], P('gx', 'gy'), may hold values from -0.046875 to 0.046875
- kv_weight: bfloat16 [18432, 512], P('gx', 'gy'), may hold values from -0.046875 to 0.046875
- ffn_weight: bfloat16 [18432, 36864], P('gx', 'gy'), may hold values from -0.046875 to 0.046875
- cache_keys: bfloat16 [128, 512, 256], P(('groups', 'gx', 'gy')), parts along dimension 0, may hold values from -520 to 520
- cache_values: bfloat16 [128, 512, 256], P(('groups', 'gx', 'gy')), parts along dimension 0, may hold values from -6 to 6
- cache_lengths: int32 [128], P(('groups', 'gx', 'gy')), parts along dimension 0, may hold values from 1 to 512, as said below
- slot_rows: int32 [128], P('groups'), parts along dimension 0, may hold values from 0 to 63, each once
Outputs:
- attended: bfloat16 [128, 6144], P(('groups', 'gx', 'gy')), parts along dimension 0
- ffn_hidden: bfloat16 [128, 36864], P(('groups', 'gx'), 'gy'), parts along dimension 0
The draws below stay inside these ranges and needn't reach their ends.
There are 2 independent parts, one for each index of `groups`. The reference program is written for one: setup_inputs(seed, part) draws one part's arguments, and reference() takes and returns one part's arrays. A program takes and returns all parts, laid end to end along the dimension named above; an argument that names none is the same for every part. Nothing has to cross between parts.
Inputs may be any that keep to these rules, and one draw needn't show every extreme that they name: `cache_lengths`: each filled length is at least 1, and some slot is full in every draw.
All inputs are finite; a program needn't handle non-finite values.
Results may differ from the reference program's by a relative error of at most 0.012.
The reference program's roundings to bfloat16 on the way (of `queries`, `new_kv` and `probs`) count: a program that leaves them out, or rounds other values in their place, can miss the bound.
Values may be sent and summed in bfloat16 or wider, within the bound.
A program may use at most 256 MiB of HBM per device.

```python
import jax
import jax.numpy as jnp

D = 18432
HEADS = 24
DH = 256
FF = 36864
CTX = 512
HQ = 6144
BATCH = 64


def draw_cache_keys(key, part):
    key = jax.random.fold_in(key, 5)
    normal_base = jnp.clip(jax.random.normal(key, (BATCH, CTX, DH), jnp.float32), -5.0, 5.0)
    return normal_base.astype(jnp.bfloat16)


def draw_cache_lengths(key, part):
    key = jax.random.fold_in(key, 11)
    length_key, full_key = jax.random.split(key)
    lengths = jax.random.randint(length_key, (BATCH,), 1, CTX + 1, jnp.int32)
    full_slot = jax.random.randint(full_key, (), 0, BATCH, jnp.int32)
    slots = jnp.arange(BATCH, dtype=jnp.int32)
    return jnp.where(slots == full_slot, CTX, lengths).astype(jnp.int32)


def strengthened(array, key, source, target, parts, factor):
    def block_of(dim):
        return (jnp.arange(array.shape[dim]) // (array.shape[dim] // parts)).reshape((-1,) + (1,) * (array.ndim - 1 - dim))

    one_side = jax.random.permutation(key, parts)[block_of(target)]
    second = (block_of(target) + parts // 2) % parts
    return jnp.where((block_of(source) == one_side) | (block_of(source) == second), factor * array, array)


def block_levels(key, extent, shards, least, largest):
    loudness = 1.0
    for axis_at, shards_of in shards:
        steps = jax.random.uniform(jax.random.fold_in(jax.random.fold_in(key, 6), axis_at), (shards_of,), jnp.float32, least / len(shards), largest / len(shards))
        loudness = loudness * jnp.repeat(jnp.exp(steps), extent[axis_at] // shards_of).reshape((-1,) + (1,) * (len(extent) - 1 - axis_at))
    return loudness


def normal_values(own_key, shape, spread, reach, cuts=(), held_as=jnp.bfloat16):
    entries = spread * jax.random.normal(own_key, shape, jnp.float32)
    if cuts:
        entries = entries * block_levels(own_key, shape, cuts, -0.22, 0.18)
    return jnp.clip(entries, -reach, reach).astype(held_as)


def gaussian_with(own_key, dims, scale, most, shards, heavy, kind=jnp.bfloat16):
    array = scale * jax.random.normal(own_key, dims, jnp.float32)
    if shards:
        array = array * block_levels(own_key, dims, shards, -0.22, 0.18)
    return jnp.clip(strengthened(array, jax.random.fold_in(own_key, 3), *heavy), -most, most).astype(kind)


def setup_inputs(seed: int = 0, part: int = 0) -> dict:
    key_of = jax.random.split(jax.random.key(seed), 9)
    part_keys = jax.random.split(jax.random.fold_in(key_of[8], part), 9)
    return {
        "activations": gaussian_with(part_keys[0], (BATCH, D), 1.0, 6.0, ((0, 4), (1, 4)), (1, 0, 4, 2.0)),
        "query_weight": normal_values(key_of[1], (D, HQ), D ** -0.5, 0.046875, ((0, 4), (1, 4))),
        "kv_weight": normal_values(key_of[2], (D, 2 * DH), D ** -0.5, 0.046875, ((0, 4), (1, 4))),
        "ffn_weight": normal_values(key_of[3], (D, FF), D ** -0.5, 0.046875, ((0, 4), (1, 4))),
        "cache_keys": draw_cache_keys(jax.random.fold_in(jax.random.fold_in(key_of[8], part), 71), part),
        "cache_values": normal_values(part_keys[5], (BATCH, CTX, DH), 1.0, 6.0, ((0, 16),)),
        "cache_lengths": draw_cache_lengths(jax.random.fold_in(jax.random.fold_in(key_of[8], part), 71), part),
        "slot_rows": jax.random.permutation(part_keys[7], BATCH).astype(jnp.int32),
    }


def attend(query_heads, new_keys, new_values, cache_keys, cache_values, cache_lengths):
    scaling = float(query_heads.shape[-1]) ** -0.5
    query_wide = query_heads.astype(jnp.float32)
    scores = jnp.einsum("rhd,rcd->rhc", query_wide, cache_keys.astype(jnp.float32)) * scaling
    new_score = jnp.einsum("rhd,rd->rh", query_wide, new_keys.astype(jnp.float32)) * scaling
    positions = jnp.arange(cache_keys.shape[1], dtype=jnp.int32)
    usable = positions[None, None, :] < cache_lengths[:, None, None]
    scores = jnp.where(usable, scores, -jnp.inf)
    peak = jnp.maximum(jnp.max(scores, axis=-1), new_score)
    weights = jnp.exp(scores - peak[..., None])
    weight_new = jnp.exp(new_score - peak)
    totals = jnp.sum(weights, axis=-1) + weight_new
    probs = (weights / totals[..., None]).astype(jnp.bfloat16)
    prob_new = (weight_new / totals).astype(jnp.bfloat16)
    result = jnp.einsum("rhc,rcd->rhd", probs.astype(jnp.float32), cache_values.astype(jnp.float32))
    result = result + prob_new.astype(jnp.float32)[..., None] * new_values.astype(jnp.float32)[:, None, :]
    return result.astype(jnp.bfloat16).reshape(query_heads.shape[0], -1)


def reference(activations, query_weight, kv_weight, ffn_weight, cache_keys, cache_values, cache_lengths, slot_rows):
    queries = jnp.dot(activations, query_weight, preferred_element_type=jnp.float32).astype(jnp.bfloat16)
    new_kv = jnp.dot(activations, kv_weight, preferred_element_type=jnp.float32).astype(jnp.bfloat16)
    ffn_hidden = jax.nn.silu(jnp.dot(activations, ffn_weight, preferred_element_type=jnp.float32)).astype(jnp.bfloat16)
    slot_queries = jnp.take(queries, slot_rows, axis=0).reshape(BATCH, HEADS, DH)
    slot_pairs = jnp.take(new_kv, slot_rows, axis=0)
    attended = attend(slot_queries, slot_pairs[:, :DH], slot_pairs[:, DH:], cache_keys, cache_values, cache_lengths)
    return attended, ffn_hidden
```

```python
import jax
import jax.numpy as jnp
from jax import lax
from jax.experimental import pallas as pl
from jax.experimental.pallas import tpu as pltpu
from jax.sharding import PartitionSpec as P

TILE = 512
SLOTS = 10
LAG = 3

DH = 256


def attend(query_heads, new_keys, new_values, cache_keys, cache_values, cache_lengths):
    scaling = float(query_heads.shape[-1]) ** (-0.5)
    scores = (
        jnp.einsum("rhd,rcd->rhc", query_heads, cache_keys, preferred_element_type=jnp.float32)
        * scaling
    )
    new_score = (
        jnp.einsum("rhd,rd->rh", query_heads, new_keys, preferred_element_type=jnp.float32)
        * scaling
    )
    positions = lax.broadcasted_iota(jnp.int32, (1, 1, cache_keys.shape[1]), 2)
    usable = positions < cache_lengths[:, None, None]
    scores = jnp.where(usable, scores, -jnp.inf)
    peak = jnp.maximum(jnp.max(scores, axis=-1), new_score)
    weights = jnp.exp(scores - peak[..., None])
    weight_new = jnp.exp(new_score - peak)
    totals = jnp.sum(weights, axis=-1) + weight_new
    probs = (weights / totals[..., None]).astype(jnp.bfloat16)
    prob_new = (weight_new / totals).astype(jnp.bfloat16)
    result = jnp.einsum("rhc,rcd->rhd", probs, cache_values, preferred_element_type=jnp.float32)
    result = (
        result
        + prob_new.astype(jnp.float32)[..., None] * new_values.astype(jnp.float32)[:, None, :]
    )
    return result.astype(jnp.bfloat16).reshape(query_heads.shape[0], -1)


def shards(
    activations,
    query_weight,
    kv_weight,
    ffn_weight,
    cache_keys,
    cache_values,
    cache_lengths,
    slot_rows,
):
    gx_count = lax.axis_size("gx")
    gy_count = lax.axis_size("gy")
    all_rows = lax.all_gather(activations, "gy", axis=0, tiled=True)
    batch_rows = all_rows.shape[0]
    per_device = batch_rows // (gx_count * gy_count)
    picked = jnp.take(all_rows, slot_rows, axis=0)
    query_part = jnp.dot(picked, query_weight, preferred_element_type=jnp.float32)
    pair_part = jnp.dot(picked, kv_weight, preferred_element_type=jnp.float32)
    query_sum, pair_sum = (
        lax.psum_scatter(query_part, "gx", scatter_dimension=0, tiled=True),
        lax.psum_scatter(pair_part, "gx", scatter_dimension=0, tiled=True),
    )
    query_own, pair_own = (
        lax.all_to_all(
            query_sum.astype(jnp.bfloat16), "gy", split_axis=0, concat_axis=1, tiled=True
        ),
        lax.all_to_all(
            pair_sum.astype(jnp.bfloat16), "gy", split_axis=0, concat_axis=1, tiled=True
        ),
    )
    head_count = query_own.shape[1] // DH
    query_heads = query_own.reshape(per_device, head_count, DH)
    attended = attend(
        query_heads, pair_own[:, :DH], pair_own[:, DH:], cache_keys, cache_values, cache_lengths
    )
    hidden_part = jnp.dot(all_rows, ffn_weight, preferred_element_type=jnp.float32)
    hidden_sum = lax.psum_scatter(hidden_part, "gx", scatter_dimension=1, tiled=True)
    activated = jax.nn.silu(hidden_sum).astype(jnp.bfloat16)
    ffn_hidden = lax.all_to_all(activated, "gx", split_axis=0, concat_axis=1, tiled=True)
    return (attended, ffn_hidden)


def send(src, dst, send_sem, recv_sem, axis, peer):
    return pltpu.make_async_remote_copy(
        src_ref=src,
        dst_ref=dst,
        send_sem=send_sem,
        recv_sem=recv_sem,
        device_id={axis: peer},
        device_id_type=pl.DeviceIdType.MESH,
    )


def project_kernel(
    act, perm, wq, wkv, wf,
    hidden_out, pairs_out,
    wbuf, kvbuf, rows, picked, part, own, fsend, frecv, qown, qsend, qrecv, pair_own, gathered,
    wsem, kvsem, a_send, a_recv, f_send, f_recv, q_send, q_recv, g_send, g_recv,
):
    gx, gy = lax.axis_index("gx"), lax.axis_index("gy")
    q_tiles = wq.shape[1] // TILE
    f_tiles = wf.shape[1] // TILE
    q_width = wq.shape[1]
    ahead = SLOTS - q_tiles
    block = act.shape[0]

    def load_q(i):
        return pltpu.make_async_copy(wq.at[:, pl.ds(i * TILE, TILE)], wbuf.at[i], wsem.at[i])

    def load_f(t):
        slot = lax.rem(t + q_tiles, SLOTS)
        columns = pl.ds(pl.multiple_of(t * TILE, TILE), TILE)
        return pltpu.make_async_copy(wf.at[:, columns], wbuf.at[slot], wsem.at[slot])

    load_kv = pltpu.make_async_copy(wkv, kvbuf, kvsem)

    for i in range(q_tiles):
        load_q(i).start()
    load_kv.start()

    barrier = pltpu.get_barrier_semaphore()
    for k in range(1, 4):
        for axis, me in (("gx", gx), ("gy", gy)):
            pl.semaphore_signal(
                barrier, inc=1, device_id={axis: lax.rem(me + k, 4)},
                device_id_type=pl.DeviceIdType.MESH,
            )
    pl.semaphore_wait(barrier, 6)

    own_rows = pl.ds(pl.multiple_of(gy * block, block), block)
    row_copies = []
    for k in (2, 1, 3):
        copy = send(
            act, rows.at[own_rows], a_send.at[k - 1], a_recv.at[k - 1], "gy", lax.rem(gy + k, 4)
        )
        copy.start()
        row_copies.append(copy)
    for t in range(ahead):
        load_f(jnp.int32(t)).start()
    rows[own_rows, :] = act[...]
    for copy in row_copies:
        copy.wait()

    picked[...] = jnp.dot(perm[...], rows[...], preferred_element_type=jnp.float32).astype(
        jnp.bfloat16
    )

    def peer_rows(k):
        return pl.ds(pl.multiple_of(lax.rem(gx + k, 4) * block, block), block)

    for i in range(q_tiles + 1):
        if i < q_tiles:
            load_q(i).wait()
            columns = slice(i * TILE, (i + 1) * TILE)
            part[...] = jnp.dot(picked[...], wbuf[i], preferred_element_type=jnp.float32)
            load_f(jnp.int32(ahead + i)).start()
            width = TILE
        else:
            load_kv.wait()
            width = kvbuf.shape[1]
            columns = slice(q_width, q_width + width)
            part[:, :width] = jnp.dot(
                picked[...], kvbuf[...], preferred_element_type=jnp.float32
            )
        qown[:, columns] = part[peer_rows(0), :width]
        for k in range(1, 4):
            qsend[k - 1, :, columns] = part[peer_rows(k), :width]
    q_copies = []
    for k in (2, 1, 3):
        copy = send(
            qsend.at[k - 1], qrecv.at[k - 1], q_send.at[k - 1], q_recv.at[k - 1],
            "gx", lax.rem(gx + k, 4),
        )
        copy.start()
        q_copies.append(copy)

    def f_copy(t, k):
        return send(
            fsend.at[t, k - 1], frecv.at[t, k - 1], f_send.at[t, k - 1], f_recv.at[t, k - 1],
            "gx", lax.rem(gx + k, 4),
        )

    def multiply(t):
        load_f(t).wait()
        slot = lax.rem(t + q_tiles, SLOTS)
        part[...] = jnp.dot(rows[...], wbuf[slot], preferred_element_type=jnp.float32)

        @pl.when(t + SLOTS < f_tiles)
        def _():
            load_f(t + SLOTS).start()

        for k in range(1, 4):
            fsend[t, k - 1] = part[peer_rows(k), :].astype(jnp.bfloat16)
            f_copy(t, k).start()
        own[t] = part[peer_rows(0), :]

    def finish(t):
        total = own[t]
        for k in range(1, 4):
            f_copy(t, k).wait()
            total = total + frecv[t, k - 1].astype(jnp.float32)
        columns = pl.ds(pl.multiple_of(t * TILE, TILE), TILE)
        hidden_out[:, columns] = (total / (1.0 + jnp.exp(-total))).astype(jnp.bfloat16)

    def first(t, carry):
        multiply(t)
        return carry

    def middle(t, carry):
        multiply(t)
        finish(t - LAG)
        return carry

    def last(t, carry):
        finish(t)
        return carry

    lax.fori_loop(0, LAG, first, 0)

    for copy in q_copies:
        copy.wait()
    pair_own[...] = (qown[...] + qrecv[0] + qrecv[1] + qrecv[2]).astype(jnp.bfloat16)
    gathered[gy] = pair_own[...]
    g_copies = []
    for k in (2, 1, 3):
        copy = send(
            pair_own, gathered.at[gy], g_send.at[k - 1], g_recv.at[k - 1],
            "gy", lax.rem(gy + k, 4),
        )
        copy.start()
        g_copies.append(copy)

    lax.fori_loop(LAG, f_tiles, middle, 0)
    for copy in g_copies:
        copy.wait()
    pairs_out[...] = gathered[...]
    lax.fori_loop(f_tiles - LAG, f_tiles, last, 0)


def project(act, perm, wq, wkv, wf):
    block, depth = act.shape
    batch = 4 * block
    f_tiles = wf.shape[1] // TILE
    width = wq.shape[1] + wkv.shape[1]
    bf16, f32 = jnp.bfloat16, jnp.float32
    dma = pltpu.SemaphoreType.DMA
    vmem = pl.BlockSpec(memory_space=pltpu.VMEM)
    hbm = pl.BlockSpec(memory_space=pl.ANY)
    return pl.pallas_call(
        project_kernel,
        out_shape=(
            jax.ShapeDtypeStruct((block, wf.shape[1]), bf16),
            jax.ShapeDtypeStruct((4, block, width), bf16),
        ),
        in_specs=[vmem, vmem, hbm, hbm, hbm],
        out_specs=(vmem, vmem),
        scratch_shapes=[
            pltpu.VMEM((SLOTS, depth, TILE), bf16),
            pltpu.VMEM((depth, wkv.shape[1]), bf16),
            pltpu.VMEM((batch, depth), bf16),
            pltpu.VMEM((batch, depth), bf16),
            pltpu.VMEM((batch, TILE), f32),
            pltpu.VMEM((f_tiles, block, TILE), f32),
            pltpu.VMEM((f_tiles, 3, block, TILE), bf16),
            pltpu.VMEM((f_tiles, 3, block, TILE), bf16),
            pltpu.VMEM((block, width), f32),
            pltpu.VMEM((3, block, width), f32),
            pltpu.VMEM((3, block, width), f32),
            pltpu.VMEM((block, width), bf16),
            pltpu.VMEM((4, block, width), bf16),
            dma((SLOTS,)),
            dma(()),
            dma((3,)),
            dma((3,)),
            dma((f_tiles, 3)),
            dma((f_tiles, 3)),
            dma((3,)),
            dma((3,)),
            dma((3,)),
            dma((3,)),
        ],
        compiler_params=pltpu.CompilerParams(
            collective_id=0, has_side_effects=True, vmem_limit_bytes=60 * 1024 * 1024
        ),
        cost_estimate=pl.CostEstimate(
            flops=2 * batch * depth * (width + wf.shape[1]),
            bytes_accessed=2 * depth * (width + wf.shape[1]),
            transcendentals=block * wf.shape[1],
        ),
    )(act, perm, wq, wkv, wf)


def fused_shards(
    activations,
    query_weight,
    kv_weight,
    ffn_weight,
    cache_keys,
    cache_values,
    cache_lengths,
    slot_rows,
):
    slots = slot_rows.shape[0]
    rows = lax.broadcasted_iota(jnp.int32, (slots, slots), 1)
    perm = (slot_rows[:, None] == rows).astype(jnp.bfloat16)
    ffn_hidden, pairs = project(activations, perm, query_weight, kv_weight, ffn_weight)
    per_device = cache_keys.shape[0]
    q_width = query_weight.shape[1]
    mine = lax.dynamic_slice_in_dim(pairs, lax.axis_index("gy") * per_device, per_device, axis=1)
    mine = mine.transpose(1, 0, 2)
    query_heads = mine[..., :q_width].reshape(per_device, -1, DH)
    pair_own = mine[..., q_width:].reshape(per_device, -1)
    attended = attend(
        query_heads, pair_own[:, :DH], pair_own[:, DH:], cache_keys, cache_values, cache_lengths
    )
    return (attended, ffn_hidden)


def solution(mesh):
    small = mesh.shape["gx"] == 4 and mesh.shape["gy"] == 4
    in_specs = (
        P(("groups", "gy"), "gx"),
        P("gx", "gy"),
        P("gx", "gy"),
        P("gx", "gy"),
        P(("groups", "gx", "gy"), None, None),
        P(("groups", "gx", "gy"), None, None),
        P(("groups", "gx", "gy")),
        P("groups"),
    )
    out_specs = (P(("groups", "gx", "gy"), None), P(("groups", "gx"), "gy"))
    body = fused_shards if small else shards
    return jax.shard_map(body, mesh=mesh, in_specs=in_specs, out_specs=out_specs, check_vma=False)
```

```python
import jax
import jax.numpy as jnp
from jax import lax
from jax.experimental import pallas as pl
from jax.experimental.pallas import tpu as pltpu
from jax.sharding import PartitionSpec as P

TILE = 512
SLOTS = 10
LAG = 3
CHUNKS = 4

DH = 256


def attend(query_heads, new_keys, new_values, cache_keys, cache_values, cache_lengths):
    scaling = float(query_heads.shape[-1]) ** (-0.5)
    scores = (
        jnp.einsum("rhd,rcd->rhc", query_heads, cache_keys, preferred_element_type=jnp.float32)
        * scaling
    )
    new_score = (
        jnp.einsum("rhd,rd->rh", query_heads, new_keys, preferred_element_type=jnp.float32)
        * scaling
    )
    positions = lax.broadcasted_iota(jnp.int32, (1, 1, cache_keys.shape[1]), 2)
    usable = positions < cache_lengths[:, None, None]
    scores = jnp.where(usable, scores, -jnp.inf)
    peak = jnp.maximum(jnp.max(scores, axis=-1), new_score)
    weights = jnp.exp(scores - peak[..., None])
    weight_new = jnp.exp(new_score - peak)
    totals = jnp.sum(weights, axis=-1) + weight_new
    probs = (weights / totals[..., None]).astype(jnp.bfloat16)
    prob_new = (weight_new / totals).astype(jnp.bfloat16)
    result = jnp.einsum("rhc,rcd->rhd", probs, cache_values, preferred_element_type=jnp.float32)
    result = (
        result
        + prob_new.astype(jnp.float32)[..., None] * new_values.astype(jnp.float32)[:, None, :]
    )
    return result.astype(jnp.bfloat16).reshape(query_heads.shape[0], -1)


def shards(
    activations,
    query_weight,
    kv_weight,
    ffn_weight,
    cache_keys,
    cache_values,
    cache_lengths,
    slot_rows,
):
    gx_count = lax.axis_size("gx")
    gy_count = lax.axis_size("gy")
    all_rows = lax.all_gather(activations, "gy", axis=0, tiled=True)
    batch_rows = all_rows.shape[0]
    per_device = batch_rows // (gx_count * gy_count)
    picked = jnp.take(all_rows, slot_rows, axis=0)
    query_part = jnp.dot(picked, query_weight, preferred_element_type=jnp.float32)
    pair_part = jnp.dot(picked, kv_weight, preferred_element_type=jnp.float32)
    query_sum, pair_sum = (
        lax.psum_scatter(query_part, "gx", scatter_dimension=0, tiled=True),
        lax.psum_scatter(pair_part, "gx", scatter_dimension=0, tiled=True),
    )
    query_own, pair_own = (
        lax.all_to_all(
            query_sum.astype(jnp.bfloat16), "gy", split_axis=0, concat_axis=1, tiled=True
        ),
        lax.all_to_all(
            pair_sum.astype(jnp.bfloat16), "gy", split_axis=0, concat_axis=1, tiled=True
        ),
    )
    head_count = query_own.shape[1] // DH
    query_heads = query_own.reshape(per_device, head_count, DH)
    attended = attend(
        query_heads, pair_own[:, :DH], pair_own[:, DH:], cache_keys, cache_values, cache_lengths
    )
    hidden_part = jnp.dot(all_rows, ffn_weight, preferred_element_type=jnp.float32)
    hidden_sum = lax.psum_scatter(hidden_part, "gx", scatter_dimension=1, tiled=True)
    activated = jax.nn.silu(hidden_sum).astype(jnp.bfloat16)
    ffn_hidden = lax.all_to_all(activated, "gx", split_axis=0, concat_axis=1, tiled=True)
    return (attended, ffn_hidden)


def send(src, dst, send_sem, recv_sem, axis, peer):
    return pltpu.make_async_remote_copy(
        src_ref=src,
        dst_ref=dst,
        send_sem=send_sem,
        recv_sem=recv_sem,
        device_id={axis: peer},
        device_id_type=pl.DeviceIdType.MESH,
    )


def project_kernel(
    act, slots, lengths, wq, wkv, wf, keys, values,
    attended_out, hidden_out,
    wbuf, kvbuf, rows, perm, acc, kv_acc, part, own, fsend, frecv, qown, qsend, qrecv, pair_own,
    gathered, wide, kbuf, vbuf, flat,
    c_sem, wsem, kvsem, cache_sem, a_send, a_recv, f_send, f_recv, q_send, q_recv, g_send, g_recv,
):
    f32, bf16 = jnp.float32, jnp.bfloat16
    gx, gy = lax.axis_index("gx"), lax.axis_index("gy")
    q_width = wq.shape[1]
    q_tiles = q_width // TILE
    f_tiles = wf.shape[1] // TILE
    ahead = SLOTS - q_tiles
    block, depth = act.shape
    chunk = depth // CHUNKS
    kv_width = kvbuf.shape[1]

    def tile_columns(t):
        return pl.ds(pl.multiple_of(t * TILE, TILE), TILE)

    def load_chunk(c, i):
        features = pl.ds(c * chunk, chunk)
        if i < q_tiles:
            source = wq.at[features, pl.ds(i * TILE, TILE)]
        else:
            source = wf.at[features, pl.ds((i - q_tiles) * TILE, TILE)]
        return pltpu.make_async_copy(source, wbuf.at[i, features], c_sem.at[c, i])

    def await_chunk(c, i):
        features = pl.ds(c * chunk, chunk)
        here = wbuf.at[i, features]
        pltpu.make_async_copy(wf.at[features, pl.ds(0, TILE)], here, c_sem.at[c, i]).wait()

    def load_f(t):
        slot = lax.rem(t + q_tiles, SLOTS)
        return pltpu.make_async_copy(wf.at[:, tile_columns(t)], wbuf.at[slot], wsem.at[slot])

    load_kv = pltpu.make_async_copy(wkv, kvbuf, kvsem)
    load_keys = pltpu.make_async_copy(keys, kbuf, cache_sem.at[0])
    load_values = pltpu.make_async_copy(values, vbuf, cache_sem.at[1])

    def start_weights(c):
        for i in range(SLOTS):
            load_chunk(c, i).start()

    barrier = pltpu.get_barrier_semaphore()
    for k in range(1, 4):
        for axis, me in (("gx", gx), ("gy", gy)):
            pl.semaphore_signal(
                barrier, inc=1, device_id={axis: lax.rem(me + k, 4)},
                device_id_type=pl.DeviceIdType.MESH,
            )
    start_weights(0)
    load_kv.start()
    pl.semaphore_wait(barrier, 6)

    own_rows = pl.ds(pl.multiple_of(gy * block, block), block)

    def row_copy(c, k):
        features = pl.ds(c * chunk, chunk)
        return send(
            act.at[:, features], rows.at[own_rows, features],
            a_send.at[c, k - 1], a_recv.at[c, k - 1], "gy", lax.rem(gy + k, 4),
        )

    def start_rows(c):
        for k in (2, 1, 3):
            row_copy(c, k).start()

    start_rows(0)
    start_rows(1)
    start_weights(1)
    rows[own_rows, :] = act[...]
    batch = rows.shape[0]
    source_row = lax.broadcasted_iota(jnp.int32, (batch, batch), 0)
    perm[...] = jnp.where(source_row == slots[...], 1.0, 0.0).astype(f32).T.astype(bf16)

    def peer_rows(k):
        return pl.ds(pl.multiple_of(lax.rem(gx + k, 4) * block, block), block)

    def f_copy(t, k):
        return send(
            fsend.at[t, k - 1], frecv.at[t, k - 1], f_send.at[t, k - 1], f_recv.at[t, k - 1],
            "gx", lax.rem(gx + k, 4),
        )

    def q_copy(k):
        return send(
            qsend.at[k - 1], qrecv.at[k - 1], q_send.at[k - 1], q_recv.at[k - 1],
            "gx", lax.rem(gx + k, 4),
        )

    def g_copy(k):
        return send(
            pair_own, gathered.at[gy], g_send.at[k - 1], g_recv.at[k - 1],
            "gy", lax.rem(gy + k, 4),
        )

    def spread(t):
        for k in range(1, 4):
            fsend[t, k - 1] = part[peer_rows(k), :].astype(bf16)
            f_copy(t, k).start()
        own[t] = part[peer_rows(0), :]

    def share_queries(width, columns):
        qown[:, columns] = part[peer_rows(0), :width]
        for k in range(1, 4):
            qsend[k - 1, :, columns] = part[peer_rows(k), :width]

    for c in range(CHUNKS):
        for k in range(1, 4):
            row_copy(c, k).wait()
        if c + 2 < CHUNKS:
            start_rows(c + 2)
            start_weights(c + 2)
        features = slice(c * chunk, (c + 1) * chunk)
        final = c == CHUNKS - 1
        if c == 0:
            load_kv.wait()
        picked = jnp.dot(perm[...], rows[:, features], preferred_element_type=f32).astype(bf16)

        def times(left, right, total, at, c=c):
            out = jnp.dot(left, right, preferred_element_type=f32)
            return out if c == 0 else total[at] + out

        for i in range(q_tiles):
            await_chunk(c, i)
            out = times(picked, wbuf[i, features, :], acc, i)
            if final:
                part[...] = out
                load_f(jnp.int32(ahead + i)).start()
                share_queries(TILE, slice(i * TILE, (i + 1) * TILE))
            else:
                acc[i] = out
        out = times(picked, kvbuf[features, :], kv_acc, Ellipsis)
        if final:
            part[:, :kv_width] = out
            share_queries(kv_width, slice(q_width, q_width + kv_width))
            for k in (2, 1, 3):
                q_copy(k).start()
        else:
            kv_acc[...] = out

        def hidden_chunk(t, carry, c=c, features=features, final=final, times=times):
            slot = t + q_tiles
            await_chunk(c, slot)
            out = times(rows[:, features], wbuf[slot, features, :], acc, slot)
            if final:
                part[...] = out

                @pl.when(t + SLOTS < f_tiles)
                def _():
                    load_f(t + SLOTS).start()

                spread(t)
            else:
                acc[slot] = out
            return carry

        lax.fori_loop(0, ahead, hidden_chunk, 0)

    def multiply(t):
        load_f(t).wait()
        slot = lax.rem(t + q_tiles, SLOTS)
        part[...] = jnp.dot(rows[...], wbuf[slot], preferred_element_type=f32)

        @pl.when(t + SLOTS < f_tiles)
        def _():
            load_f(t + SLOTS).start()

        spread(t)

    def finish(t):
        total = own[t]
        for k in range(1, 4):
            f_copy(t, k).wait()
            total = total + frecv[t, k - 1].astype(f32)
        hidden_out[:, tile_columns(t)] = (total / (1.0 + jnp.exp(-total))).astype(bf16)

    def doubled(t, carry):
        multiply(t)
        finish(2 * (t - ahead))
        finish(2 * (t - ahead) + 1)
        return carry

    def middle(t, carry):
        multiply(t)
        finish(t - LAG)
        return carry

    def last(t, carry):
        finish(t)
        return carry

    load_keys.start()
    load_values.start()
    even = ahead + ahead - LAG
    lax.fori_loop(ahead, even, doubled, 0)

    for k in range(1, 4):
        q_copy(k).wait()
    pair_own[...] = (qown[...] + qrecv[0] + qrecv[1] + qrecv[2]).astype(bf16)
    gathered[gy] = pair_own[...]
    for k in (2, 1, 3):
        g_copy(k).start()

    lax.fori_loop(even, f_tiles - 2, middle, 0)

    for k in range(1, 4):
        g_copy(k).wait()
    wide[...] = gathered[...].astype(f32)
    load_keys.wait()
    load_values.wait()
    count, positions = kbuf.shape[0], kbuf.shape[1]
    heads = q_width // DH
    scaling = float(DH) ** (-0.5)
    for i in range(count):
        at = pl.ds(gy * count + i, 1)
        line = [wide[source, at, :] for source in range(4)]
        query = jnp.concatenate(
            [line[n][:, h * DH : (h + 1) * DH] for n in range(4) for h in range(heads)], axis=0
        )
        pair = jnp.concatenate([line[n][:, q_width:] for n in range(4)], axis=1)
        new_key, new_value = pair[:, :DH], pair[:, DH:]
        scores = scaling * lax.dot_general(
            query.astype(bf16), kbuf[i], (((1,), (1,)), ((), ())), preferred_element_type=f32
        )
        new_score = jnp.sum(query * new_key, axis=1, keepdims=True) * scaling
        usable = lax.broadcasted_iota(jnp.int32, scores.shape, 1) < lengths[i]
        scores = jnp.where(usable, scores, -jnp.inf)
        peak = jnp.maximum(jnp.max(scores, axis=1, keepdims=True), new_score)
        weights = jnp.exp(scores - peak)
        weight_new = jnp.exp(new_score - peak)
        totals = jnp.sum(weights, axis=1, keepdims=True) + weight_new
        probs = (weights / totals).astype(bf16)
        prob_new = (weight_new / totals).astype(bf16).astype(f32)
        result = jnp.dot(probs, vbuf[i], preferred_element_type=f32) + prob_new * new_value
        for h in range(4 * heads):
            flat[i : i + 1, h * DH : (h + 1) * DH] = result[h : h + 1, :]
    attended_out[...] = flat[...].astype(bf16)

    lax.fori_loop(f_tiles - 2, f_tiles, middle, 0)
    lax.fori_loop(f_tiles - LAG, f_tiles, last, 0)


def fused_shards(
    activations,
    query_weight,
    kv_weight,
    ffn_weight,
    cache_keys,
    cache_values,
    cache_lengths,
    slot_rows,
):
    block, depth = activations.shape
    batch = slot_rows.shape[0]
    hidden = ffn_weight.shape[1]
    f_tiles = hidden // TILE
    kv_width = kv_weight.shape[1]
    width = query_weight.shape[1] + kv_width
    count = cache_keys.shape[0]
    features = 4 * query_weight.shape[1]
    bf16, f32 = jnp.bfloat16, jnp.float32
    dma = pltpu.SemaphoreType.DMA
    vmem = pl.BlockSpec(memory_space=pltpu.VMEM)
    smem = pl.BlockSpec(memory_space=pltpu.SMEM)
    hbm = pl.BlockSpec(memory_space=pl.ANY)
    return pl.pallas_call(
        project_kernel,
        out_shape=(
            jax.ShapeDtypeStruct((count, features), bf16),
            jax.ShapeDtypeStruct((block, hidden), bf16),
        ),
        in_specs=[vmem, vmem, smem, hbm, hbm, hbm, hbm, hbm],
        out_specs=(vmem, vmem),
        scratch_shapes=[
            pltpu.VMEM((SLOTS, depth, TILE), bf16),
            pltpu.VMEM((depth, kv_width), bf16),
            pltpu.VMEM((batch, depth), bf16),
            pltpu.VMEM((batch, batch), bf16),
            pltpu.VMEM((SLOTS, batch, TILE), f32),
            pltpu.VMEM((batch, kv_width), f32),
            pltpu.VMEM((batch, TILE), f32),
            pltpu.VMEM((f_tiles, block, TILE), f32),
            pltpu.VMEM((f_tiles, 3, block, TILE), bf16),
            pltpu.VMEM((f_tiles, 3, block, TILE), bf16),
            pltpu.VMEM((block, width), f32),
            pltpu.VMEM((3, block, width), f32),
            pltpu.VMEM((3, block, width), f32),
            pltpu.VMEM((block, width), bf16),
            pltpu.VMEM((4, block, width), bf16),
            pltpu.VMEM((4, block, width), f32),
            pltpu.VMEM(cache_keys.shape, bf16),
            pltpu.VMEM(cache_values.shape, bf16),
            pltpu.VMEM((count, features), f32),
            dma((CHUNKS, SLOTS)),
            dma((SLOTS,)),
            dma(()),
            dma((2,)),
            dma((CHUNKS, 3)),
            dma((CHUNKS, 3)),
            dma((f_tiles, 3)),
            dma((f_tiles, 3)),
            dma((3,)),
            dma((3,)),
            dma((3,)),
            dma((3,)),
        ],
        compiler_params=pltpu.CompilerParams(
            collective_id=0, has_side_effects=True, vmem_limit_bytes=61 * 1024 * 1024
        ),
        cost_estimate=pl.CostEstimate(
            flops=2 * batch * depth * (width + hidden),
            bytes_accessed=2 * depth * (width + hidden),
            transcendentals=block * hidden,
        ),
    )(
        activations, slot_rows.reshape(1, batch), cache_lengths,
        query_weight, kv_weight, ffn_weight, cache_keys, cache_values,
    )


def solution(mesh):
    small = mesh.shape["gx"] == 4 and mesh.shape["gy"] == 4
    in_specs = (
        P(("groups", "gy"), "gx"),
        P("gx", "gy"),
        P("gx", "gy"),
        P("gx", "gy"),
        P(("groups", "gx", "gy"), None, None),
        P(("groups", "gx", "gy"), None, None),
        P(("groups", "gx", "gy")),
        P("groups"),
    )
    out_specs = (P(("groups", "gx", "gy"), None), P(("groups", "gx"), "gy"))
    body = fused_shards if small else shards
    return jax.shard_map(body, mesh=mesh, in_specs=in_specs, out_specs=out_specs, check_vma=False)
```

```python
import jax
import jax.numpy as jnp
from jax import lax
from jax.experimental import pallas as pl
from jax.experimental.pallas import tpu as pltpu
from jax.sharding import PartitionSpec as P

TILE = 512
SLOTS = 10
LAG = 3
CHUNKS = 4

DH = 256


def attend(query_heads, new_keys, new_values, cache_keys, cache_values, cache_lengths):
    scaling = float(query_heads.shape[-1]) ** (-0.5)
    scores = (
        jnp.einsum("rhd,rcd->rhc", query_heads, cache_keys, preferred_element_type=jnp.float32)
        * scaling
    )
    new_score = (
        jnp.einsum("rhd,rd->rh", query_heads, new_keys, preferred_element_type=jnp.float32)
        * scaling
    )
    positions = lax.broadcasted_iota(jnp.int32, (1, 1, cache_keys.shape[1]), 2)
    usable = positions < cache_lengths[:, None, None]
    scores = jnp.where(usable, scores, -jnp.inf)
    peak = jnp.maximum(jnp.max(scores, axis=-1), new_score)
    weights = jnp.exp(scores - peak[..., None])
    weight_new = jnp.exp(new_score - peak)
    totals = jnp.sum(weights, axis=-1) + weight_new
    probs = (weights / totals[..., None]).astype(jnp.bfloat16)
    prob_new = (weight_new / totals).astype(jnp.bfloat16)
    result = jnp.einsum("rhc,rcd->rhd", probs, cache_values, preferred_element_type=jnp.float32)
    result = (
        result
        + prob_new.astype(jnp.float32)[..., None] * new_values.astype(jnp.float32)[:, None, :]
    )
    return result.astype(jnp.bfloat16).reshape(query_heads.shape[0], -1)


def shards(
    activations,
    query_weight,
    kv_weight,
    ffn_weight,
    cache_keys,
    cache_values,
    cache_lengths,
    slot_rows,
):
    gx_count = lax.axis_size("gx")
    gy_count = lax.axis_size("gy")
    all_rows = lax.all_gather(activations, "gy", axis=0, tiled=True)
    batch_rows = all_rows.shape[0]
    per_device = batch_rows // (gx_count * gy_count)
    picked = jnp.take(all_rows, slot_rows, axis=0)
    query_part = jnp.dot(picked, query_weight, preferred_element_type=jnp.float32)
    pair_part = jnp.dot(picked, kv_weight, preferred_element_type=jnp.float32)
    query_sum, pair_sum = (
        lax.psum_scatter(query_part, "gx", scatter_dimension=0, tiled=True),
        lax.psum_scatter(pair_part, "gx", scatter_dimension=0, tiled=True),
    )
    query_own, pair_own = (
        lax.all_to_all(
            query_sum.astype(jnp.bfloat16), "gy", split_axis=0, concat_axis=1, tiled=True
        ),
        lax.all_to_all(
            pair_sum.astype(jnp.bfloat16), "gy", split_axis=0, concat_axis=1, tiled=True
        ),
    )
    head_count = query_own.shape[1] // DH
    query_heads = query_own.reshape(per_device, head_count, DH)
    attended = attend(
        query_heads, pair_own[:, :DH], pair_own[:, DH:], cache_keys, cache_values, cache_lengths
    )
    hidden_part = jnp.dot(all_rows, ffn_weight, preferred_element_type=jnp.float32)
    hidden_sum = lax.psum_scatter(hidden_part, "gx", scatter_dimension=1, tiled=True)
    activated = jax.nn.silu(hidden_sum).astype(jnp.bfloat16)
    ffn_hidden = lax.all_to_all(activated, "gx", split_axis=0, concat_axis=1, tiled=True)
    return (attended, ffn_hidden)


def send(src, dst, send_sem, recv_sem, axis, peer):
    return pltpu.make_async_remote_copy(
        src_ref=src,
        dst_ref=dst,
        send_sem=send_sem,
        recv_sem=recv_sem,
        device_id={axis: peer},
        device_id_type=pl.DeviceIdType.MESH,
    )


def project_kernel(
    act, slots, lengths, wq, wkv, wf, keys, values,
    attended_out, hidden_out,
    wbuf, kvbuf, rows, perm, acc, kv_acc, part, own, fsend, frecv, qown, qsend, qrecv, pair_own,
    gathered, wide, kbuf, vbuf, flat,
    c_sem, wsem, kvsem, cache_sem, a_send, a_recv, f_send, f_recv, q_send, q_recv, g_send, g_recv,
):
    f32, bf16 = jnp.float32, jnp.bfloat16
    gx, gy = lax.axis_index("gx"), lax.axis_index("gy")
    q_width = wq.shape[1]
    q_tiles = q_width // TILE
    f_tiles = wf.shape[1] // TILE
    ahead = SLOTS - q_tiles
    block, depth = act.shape
    chunk = depth // CHUNKS
    kv_width = kvbuf.shape[1]

    def tile_columns(t):
        return pl.ds(pl.multiple_of(t * TILE, TILE), TILE)

    def load_chunk(c, i):
        features = pl.ds(c * chunk, chunk)
        if i < q_tiles:
            source = wq.at[features, pl.ds(i * TILE, TILE)]
        else:
            source = wf.at[features, pl.ds((i - q_tiles) * TILE, TILE)]
        return pltpu.make_async_copy(source, wbuf.at[i, features], c_sem.at[c, i])

    def await_chunk(c, i):
        features = pl.ds(c * chunk, chunk)
        here = wbuf.at[i, features]
        pltpu.make_async_copy(wf.at[features, pl.ds(0, TILE)], here, c_sem.at[c, i]).wait()

    def load_f(t):
        slot = lax.rem(t + q_tiles, SLOTS)
        return pltpu.make_async_copy(wf.at[:, tile_columns(t)], wbuf.at[slot], wsem.at[slot])

    load_kv = pltpu.make_async_copy(wkv, kvbuf, kvsem)
    load_keys = pltpu.make_async_copy(keys, kbuf, cache_sem.at[0])
    load_values = pltpu.make_async_copy(values, vbuf, cache_sem.at[1])

    def start_weights(c):
        for i in range(SLOTS):
            load_chunk(c, i).start()

    barrier = pltpu.get_barrier_semaphore()
    for k in range(1, 4):
        for axis, me in (("gx", gx), ("gy", gy)):
            pl.semaphore_signal(
                barrier, inc=1, device_id={axis: lax.rem(me + k, 4)},
                device_id_type=pl.DeviceIdType.MESH,
            )
    start_weights(0)
    load_kv.start()
    pl.semaphore_wait(barrier, 6)

    own_rows = pl.ds(pl.multiple_of(gy * block, block), block)

    def row_copy(c, k):
        features = pl.ds(c * chunk, chunk)
        return send(
            act.at[:, features], rows.at[own_rows, features],
            a_send.at[c, k - 1], a_recv.at[c, k - 1], "gy", lax.rem(gy + k, 4),
        )

    def start_rows(c):
        for k in (2, 1, 3):
            row_copy(c, k).start()

    start_rows(0)
    start_rows(1)
    start_weights(1)
    rows[own_rows, :] = act[...]
    batch = rows.shape[0]
    source_row = lax.broadcasted_iota(jnp.int32, (batch, batch), 0)
    perm[...] = jnp.where(source_row == slots[...], 1.0, 0.0).astype(f32).T.astype(bf16)

    def peer_rows(k):
        return pl.ds(pl.multiple_of(lax.rem(gx + k, 4) * block, block), block)

    def f_copy(t, k):
        return send(
            fsend.at[t, k - 1], frecv.at[t, k - 1], f_send.at[t, k - 1], f_recv.at[t, k - 1],
            "gx", lax.rem(gx + k, 4),
        )

    def q_copy(k):
        return send(
            qsend.at[k - 1], qrecv.at[k - 1], q_send.at[k - 1], q_recv.at[k - 1],
            "gx", lax.rem(gx + k, 4),
        )

    def g_copy(k):
        return send(
            pair_own, gathered.at[gy], g_send.at[k - 1], g_recv.at[k - 1],
            "gy", lax.rem(gy + k, 4),
        )

    def spread(t):
        for k in range(1, 4):
            fsend[t, k - 1] = part[peer_rows(k), :].astype(bf16)
            f_copy(t, k).start()
        own[t] = part[peer_rows(0), :]

    def share_queries(width, columns):
        qown[:, columns] = part[peer_rows(0), :width]
        for k in range(1, 4):
            qsend[k - 1, :, columns] = part[peer_rows(k), :width]

    for c in range(CHUNKS):
        for k in range(1, 4):
            row_copy(c, k).wait()
        if c + 2 < CHUNKS:
            start_rows(c + 2)
            start_weights(c + 2)
        features = slice(c * chunk, (c + 1) * chunk)
        final = c == CHUNKS - 1
        if c == 0:
            load_kv.wait()
        picked = jnp.dot(perm[...], rows[:, features], preferred_element_type=f32).astype(bf16)

        def times(left, right, total, at, c=c):
            out = jnp.dot(left, right, preferred_element_type=f32)
            return out if c == 0 else total[at] + out

        for i in range(q_tiles):
            await_chunk(c, i)
            out = times(picked, wbuf[i, features, :], acc, i)
            if final:
                part[...] = out
                load_f(jnp.int32(ahead + i)).start()
                share_queries(TILE, slice(i * TILE, (i + 1) * TILE))
            else:
                acc[i] = out
        out = times(picked, kvbuf[features, :], kv_acc, Ellipsis)
        if final:
            part[:, :kv_width] = out
            share_queries(kv_width, slice(q_width, q_width + kv_width))
            for k in (2, 1, 3):
                q_copy(k).start()
        else:
            kv_acc[...] = out

        def hidden_chunk(t, carry, c=c, features=features, final=final, times=times):
            slot = t + q_tiles
            await_chunk(c, slot)
            out = times(rows[:, features], wbuf[slot, features, :], acc, slot)
            if final:
                part[...] = out

                @pl.when(t + SLOTS < f_tiles)
                def _():
                    load_f(t + SLOTS).start()

                spread(t)
            else:
                acc[slot] = out
            return carry

        lax.fori_loop(0, ahead, hidden_chunk, 0)

    def multiply(t):
        load_f(t).wait()
        slot = lax.rem(t + q_tiles, SLOTS)
        part[...] = jnp.dot(rows[...], wbuf[slot], preferred_element_type=f32)

        @pl.when(t + SLOTS < f_tiles)
        def _():
            load_f(t + SLOTS).start()

        spread(t)

    def finish(t):
        total = own[t]
        for k in range(1, 4):
            f_copy(t, k).wait()
            total = total + frecv[t, k - 1].astype(f32)
        hidden_out[:, tile_columns(t)] = (total / (1.0 + jnp.exp(-total))).astype(bf16)

    def doubled(t, carry):
        multiply(t)
        finish(2 * (t - even))
        finish(2 * (t - even) + 1)
        return carry

    def plain(t, carry):
        multiply(t)
        return carry

    def last(t, carry):
        finish(t)
        return carry

    load_keys.start()
    load_values.start()
    even = ahead + ahead - LAG
    lax.fori_loop(ahead, even, plain, 0)

    for k in range(1, 4):
        q_copy(k).wait()
    pair_own[...] = (qown[...] + qrecv[0] + qrecv[1] + qrecv[2]).astype(bf16)
    gathered[gy] = pair_own[...]
    for k in (2, 1, 3):
        g_copy(k).start()

    lax.fori_loop(even, f_tiles - 2, doubled, 0)

    for k in range(1, 4):
        g_copy(k).wait()
    wide[...] = gathered[...].astype(f32)
    load_keys.wait()
    load_values.wait()
    count, positions = kbuf.shape[0], kbuf.shape[1]
    heads = q_width // DH
    scaling = float(DH) ** (-0.5)
    for i in range(count):
        at = pl.ds(gy * count + i, 1)
        line = [wide[source, at, :] for source in range(4)]
        query = jnp.concatenate(
            [line[n][:, h * DH : (h + 1) * DH] for n in range(4) for h in range(heads)], axis=0
        )
        pair = jnp.concatenate([line[n][:, q_width:] for n in range(4)], axis=1)
        new_key, new_value = pair[:, :DH], pair[:, DH:]
        scores = scaling * lax.dot_general(
            query.astype(bf16), kbuf[i], (((1,), (1,)), ((), ())), preferred_element_type=f32
        )
        new_score = jnp.sum(query * new_key, axis=1, keepdims=True) * scaling
        usable = lax.broadcasted_iota(jnp.int32, scores.shape, 1) < lengths[i]
        scores = jnp.where(usable, scores, -jnp.inf)
        peak = jnp.maximum(jnp.max(scores, axis=1, keepdims=True), new_score)
        weights = jnp.exp(scores - peak)
        weight_new = jnp.exp(new_score - peak)
        totals = jnp.sum(weights, axis=1, keepdims=True) + weight_new
        probs = (weights / totals).astype(bf16)
        prob_new = (weight_new / totals).astype(bf16).astype(f32)
        result = jnp.dot(probs, vbuf[i], preferred_element_type=f32) + prob_new * new_value
        for h in range(4 * heads):
            flat[i : i + 1, h * DH : (h + 1) * DH] = result[h : h + 1, :]
    attended_out[...] = flat[...].astype(bf16)

    lax.fori_loop(f_tiles - 2, f_tiles, doubled, 0)
    lax.fori_loop(2 * (f_tiles - even), f_tiles, last, 0)


def fused_shards(
    activations,
    query_weight,
    kv_weight,
    ffn_weight,
    cache_keys,
    cache_values,
    cache_lengths,
    slot_rows,
):
    block, depth = activations.shape
    batch = slot_rows.shape[0]
    hidden = ffn_weight.shape[1]
    f_tiles = hidden // TILE
    kv_width = kv_weight.shape[1]
    width = query_weight.shape[1] + kv_width
    count = cache_keys.shape[0]
    features = 4 * query_weight.shape[1]
    bf16, f32 = jnp.bfloat16, jnp.float32
    dma = pltpu.SemaphoreType.DMA
    vmem = pl.BlockSpec(memory_space=pltpu.VMEM)
    smem = pl.BlockSpec(memory_space=pltpu.SMEM)
    hbm = pl.BlockSpec(memory_space=pl.ANY)
    return pl.pallas_call(
        project_kernel,
        out_shape=(
            jax.ShapeDtypeStruct((count, features), bf16),
            jax.ShapeDtypeStruct((block, hidden), bf16),
        ),
        in_specs=[vmem, vmem, smem, hbm, hbm, hbm, hbm, hbm],
        out_specs=(vmem, vmem),
        scratch_shapes=[
            pltpu.VMEM((SLOTS, depth, TILE), bf16),
            pltpu.VMEM((depth, kv_width), bf16),
            pltpu.VMEM((batch, depth), bf16),
            pltpu.VMEM((batch, batch), bf16),
            pltpu.VMEM((SLOTS, batch, TILE), f32),
            pltpu.VMEM((batch, kv_width), f32),
            pltpu.VMEM((batch, TILE), f32),
            pltpu.VMEM((f_tiles, block, TILE), f32),
            pltpu.VMEM((f_tiles, 3, block, TILE), bf16),
            pltpu.VMEM((f_tiles, 3, block, TILE), bf16),
            pltpu.VMEM((block, width), f32),
            pltpu.VMEM((3, block, width), f32),
            pltpu.VMEM((3, block, width), f32),
            pltpu.VMEM((block, width), bf16),
            pltpu.VMEM((4, block, width), bf16),
            pltpu.VMEM((4, block, width), f32),
            pltpu.VMEM(cache_keys.shape, bf16),
            pltpu.VMEM(cache_values.shape, bf16),
            pltpu.VMEM((count, features), f32),
            dma((CHUNKS, SLOTS)),
            dma((SLOTS,)),
            dma(()),
            dma((2,)),
            dma((CHUNKS, 3)),
            dma((CHUNKS, 3)),
            dma((f_tiles, 3)),
            dma((f_tiles, 3)),
            dma((3,)),
            dma((3,)),
            dma((3,)),
            dma((3,)),
        ],
        compiler_params=pltpu.CompilerParams(
            collective_id=0, has_side_effects=True, vmem_limit_bytes=61 * 1024 * 1024
        ),
        cost_estimate=pl.CostEstimate(
            flops=2 * batch * depth * (width + hidden),
            bytes_accessed=2 * depth * (width + hidden),
            transcendentals=block * hidden,
        ),
    )(
        activations, slot_rows.reshape(1, batch), cache_lengths,
        query_weight, kv_weight, ffn_weight, cache_keys, cache_values,
    )


def solution(mesh):
    small = mesh.shape["gx"] == 4 and mesh.shape["gy"] == 4
    in_specs = (
        P(("groups", "gy"), "gx"),
        P("gx", "gy"),
        P("gx", "gy"),
        P("gx", "gy"),
        P(("groups", "gx", "gy"), None, None),
        P(("groups", "gx", "gy"), None, None),
        P(("groups", "gx", "gy")),
        P("groups"),
    )
    out_specs = (P(("groups", "gx", "gy"), None), P(("groups", "gx"), "gy"))
    body = fused_shards if small else shards
    return jax.shard_map(body, mesh=mesh, in_specs=in_specs, out_specs=out_specs, check_vma=False)
```
